512 devices in a mesh: heads: 8 (over x, y_lo), seq: 64 (over z, y_hi, core).
Axes of the slice: x: 4, y: 4 (y_hi: 2, y_lo: 2; y = y_hi * 2 + y_lo), z: 16, core: 2. Of those that a mesh axis runs over, the one named last changes fastest.
Arguments:
- query_nope: bfloat16 [1, 4, 128, 128], P(None, None, 'heads'), may hold values from -6 to 6
- query_rope: bfloat16 [1, 4, 128, 64], P(None, None, 'heads'), may hold values from -8 to 8
- latent_cache: bfloat16 [1, 32768, 512], P(None, 'seq'), may hold values from -6 to 6
- rope_keys: bfloat16 [1, 64, 32768], P(None, None, 'seq'), may hold values from -8 to 8
- lengths: int32 [1], replicated, may hold values from 2 to 32765, as said below
- key_quant: bfloat16 [128, 512, 128], P('heads', 'seq'), may hold values from -127 to 127, as said below
- key_scale: float32 [128, 4], P('heads'), may hold values from 0.0006 to 0.0024
- value_quant: bfloat16 [128, 512, 128], P('heads', 'seq'), may hold values from -127 to 127, as said below
- value_scale: float32 [128, 4], P('heads'), may hold values from 0.0003 to 0.0012
- out_weight: bfloat16 [16384, 7168], P('heads', 'seq'), may hold values from -0.375 to 0.375
Outputs:
- attn_out: bfloat16 [1, 4, 7168], P(None, None, 'seq')
The draws below stay inside these ranges and needn't reach their ends.
Inputs may be any that keep to these rules, and one draw needn't show every extreme that they name: `key_quant`: whole numbers. `value_quant`: whole numbers. `lengths`: one sequence has the largest allowed length, so that its last draft token sees all 32768 positions.
All inputs are finite; a program needn't handle non-finite values.
Results may differ from the reference program's by a relative error of at most 0.019.
Values may be sent and summed in bfloat16 or wider, within the bound.
No kernel may reach another device: no remote copies, remote signals or barrier semaphores. Data moves between devices by JAX's collectives and lax.ppermute only.
A program may use at most 64 MiB of HBM per device.

```python
import math
import jax
import jax.numpy as jnp
from jax import lax

H = 128
C = 512
R = 64
NOPE = 128
V = 128
D = 7168
QB = 128
B = 1
QT = 4
CTX_DEV = 512
CONTEXT = 32768
N_SEQ = 64


def rope_pair(key):
    base_key = jax.random.fold_in(key, 911)
    key_query, key_cache = jax.random.split(base_key, 2)
    queries = jnp.clip(jax.random.normal(key_query, (B, QT, H, R), jnp.float32), -8.0, 8.0)
    keys_out = jnp.clip(jax.random.normal(key_cache, (B, R, CONTEXT), jnp.float32), -8.0, 8.0)
    return (queries, keys_out)


def draw_query_rope(key, part):
    return rope_pair(key)[0].astype(jnp.bfloat16)


def draw_rope_keys(key, part):
    return rope_pair(key)[1].astype(jnp.bfloat16)


def draw_lengths(key, part):
    values = jax.random.randint(jax.random.fold_in(key, 3), (B,), 2, CONTEXT - QT + 2)
    longest = jax.random.randint(jax.random.fold_in(key, 5), (), 0, B)
    return jnp.where(jnp.arange(B) == longest, CONTEXT - QT + 1, values).astype(jnp.int32)


def draw_key_quant(key, part):
    values = jax.random.randint(jax.random.fold_in(key, 7), (H, C, NOPE), -127, 128)
    return values.astype(jnp.float32).astype(jnp.bfloat16)


def draw_value_quant(key, part):
    values = jax.random.randint(jax.random.fold_in(key, 11), (H, C, V), -127, 128)
    return values.astype(jnp.float32).astype(jnp.bfloat16)


def steps_of(own_key, dims, cuts, least, high):
    factor_of = 1.0
    for dim, shards_of in cuts:
        draws = jax.random.uniform(jax.random.fold_in(jax.random.fold_in(own_key, 6), dim), (shards_of,), jnp.float32, least / len(cuts), high / len(cuts))
        factor_of = factor_of * jnp.repeat(jnp.exp(draws), dims[dim] // shards_of).reshape((-1,) + (1,) * (len(dims) - 1 - dim))
    return factor_of


def normal_values(own_key, shape, spread, limit, cuts=(), held_as=jnp.bfloat16):
    drawn = spread * jax.random.normal(own_key, shape, jnp.float32)
    if cuts:
        drawn = drawn * steps_of(own_key, shape, cuts, -0.22, 0.18)
    return jnp.clip(drawn, -limit, limit).astype(held_as)


def setup_inputs(seed: int = 0) -> dict:
    seeds = jax.random.split(jax.random.key(seed), 11)
    return {
        "query_nope": normal_values(seeds[0], (B, QT, H, NOPE), 1.0, 6.0, ((2, 8),)),
        "query_rope": draw_query_rope(jax.random.fold_in(seeds[10], 71), 0),
        "latent_cache": normal_values(seeds[2], (B, CONTEXT, C), 1.0, 6.0, ((1, 64),)),
        "rope_keys": draw_rope_keys(jax.random.fold_in(seeds[10], 71), 0),
        "lengths": draw_lengths(jax.random.fold_in(seeds[10], 71), 0),
        "key_quant": draw_key_quant(jax.random.fold_in(seeds[10], 71), 0),
        "key_scale": jnp.clip(jnp.exp(math.log(0.0024) - 1.3862944 * jax.random.uniform(seeds[6], (H, C // QB), jnp.float32) ** steps_of(seeds[6], (H, C // QB), ((0, 8),), -0.2, 0.2)), 0.0006, 0.0024),
        "value_quant": draw_value_quant(jax.random.fold_in(seeds[10], 71), 0),
        "value_scale": jnp.clip(jnp.exp(math.log(0.0012) - 1.3862944 * jax.random.uniform(seeds[8], (H, C // QB), jnp.float32) ** steps_of(seeds[8], (H, C // QB), ((0, 8),), -0.2, 0.2)), 0.0003, 0.0012),
        "out_weight": normal_values(seeds[9], (H * V, D), (H * V // 64) ** -0.5, 0.375, ((0, 8), (1, 64))),
    }


neg_large = -1.0e30


def expand_scales(block_scale, offset, count):
    row_ids = (offset + jnp.arange(count, dtype=jnp.int32)) // QB
    onehot = (row_ids[:, None] == jnp.arange(block_scale.shape[1], dtype=jnp.int32)[None, :]).astype(block_scale.dtype)
    return jnp.sum(block_scale[:, None, :] * onehot[None, :, :], axis=2)


def dequantize(quantized, block_scale, offset):
    factors = expand_scales(block_scale, offset, quantized.shape[1])
    return (quantized.astype(jnp.float32) * factors[:, :, None]).astype(jnp.bfloat16)


def combine(earlier, later):
    max_a, sum_a, out_a = earlier
    max_b, sum_b, out_b = later
    joint = jnp.maximum(max_a, max_b)
    fac_a = jnp.exp(max_a - joint)
    fac_b = jnp.exp(max_b - joint)
    return joint, sum_a * fac_a + sum_b * fac_b, out_a * fac_a[..., None] + out_b * fac_b[..., None]


def reference(query_nope, query_rope, latent_cache, rope_keys, lengths, key_quant, key_scale, value_quant, value_scale, out_weight):
    key_weight = dequantize(key_quant, key_scale, 0)
    value_weight = dequantize(value_quant, value_scale, 0)
    query_latent = jnp.einsum("btkn,kcn->btkc", query_nope.astype(jnp.float32), key_weight.astype(jnp.float32)).astype(jnp.bfloat16)
    factor = (NOPE + R) ** -0.5
    horizon = lengths[:, None] + jnp.arange(QT, dtype=jnp.int32)[None, :]
    lat_f = query_latent.astype(jnp.float32)
    rope_f = query_rope.astype(jnp.float32)

    def one_block(state_acc, block_idx):
        offset = (block_idx * CTX_DEV).astype(jnp.int32)
        cache_blk = lax.dynamic_slice_in_dim(latent_cache, offset, CTX_DEV, 1).astype(jnp.float32)
        rope_blk = lax.dynamic_slice_in_dim(rope_keys, offset, CTX_DEV, 2).astype(jnp.float32)
        scores = (jnp.einsum("btkc,bsc->btks", lat_f, cache_blk) + jnp.einsum("btkr,brs->btks", rope_f, rope_blk)) * factor
        position = offset + jnp.arange(CTX_DEV, dtype=jnp.int32)
        visible = (position[None, None, :] < horizon[:, :, None])[:, :, None, :]
        block_max = jnp.max(jnp.where(visible, scores, neg_large), axis=3)
        probs = jnp.where(visible, jnp.exp(scores - block_max[..., None]), 0.0)
        block_sum = jnp.sum(probs, axis=3)
        probs_bf = probs.astype(jnp.bfloat16)
        block_out = jnp.einsum("btks,bsc->btkc", probs_bf.astype(jnp.float32), cache_blk)
        return combine(state_acc, (block_max, block_sum, block_out)), None

    start_state = (jnp.full((B, QT, H), neg_large, jnp.float32), jnp.zeros((B, QT, H), jnp.float32), jnp.zeros((B, QT, H, C), jnp.float32))
    final_state, _ = lax.scan(one_block, start_state, jnp.arange(N_SEQ, dtype=jnp.int32))
    out_latent = (final_state[2] / final_state[1][..., None]).astype(jnp.bfloat16)
    head_output = jnp.einsum("btkc,kcv->btkv", out_latent.astype(jnp.float32), value_weight.astype(jnp.float32)).astype(jnp.bfloat16)
    summed = jnp.dot(head_output.reshape(B * QT, H * V), out_weight, preferred_element_type=jnp.float32)
    return summed.astype(jnp.bfloat16).reshape(B, QT, D)
```

```python
import jax
import jax.numpy as jnp
from jax import lax
from jax.experimental import pallas as pl
from jax.experimental.pallas import tpu as pltpu
from jax.sharding import Mesh, PartitionSpec as P

QB = 128
RUN = 16
LANES = 128
NEG = -1e30
F32 = jnp.float32
BF16 = jnp.bfloat16
SMEM = pl.BlockSpec(memory_space=pltpu.SMEM)
HBM = pl.BlockSpec(memory_space=pltpu.HBM)
VMEM = pl.BlockSpec(memory_space=pltpu.VMEM)


def iota(shape, dim):
    return lax.broadcasted_iota(jnp.int32, shape, dim)


def dot(a, b, dims=((1,), (0,))):
    return lax.dot_general(a, b, (dims, ((), ())), preferred_element_type=F32)


def head_major(drafts, heads, copies):
    rows = drafts * heads
    col = iota((rows, copies * rows), 1) % rows
    source = (col % drafts) * heads + col // drafts
    return (iota((rows, copies * rows), 0) == source).astype(BF16)


def query_kernel(block_ref, scale_hbm, query_hbm, quant_hbm, out_ref, scale_ref, query_ref, quant_ref, sems):
    copies = [
        pltpu.make_async_copy(source, target, sems.at[k])
        for k, (source, target) in enumerate(
            ((quant_hbm, quant_ref), (query_hbm, query_ref), (scale_hbm, scale_ref))
        )
    ]
    for copy in copies:
        copy.start()
    for copy in copies:
        copy.wait()
    heads, cols, width = quant_ref.shape
    rows = query_ref.shape[0]
    block = block_ref[0]
    weight = jnp.concatenate(
        [(quant_ref[h].astype(F32) * scale_ref[block, h]).astype(BF16) for h in range(heads)], axis=0
    )
    both = dot(weight, query_ref[...], ((1,), (1,)))
    own = iota(both.shape, 0) // cols == iota(both.shape, 1) % heads
    piece = jnp.sum(jnp.where(own, both, 0.0).reshape(heads, cols, rows), axis=0)
    moved = dot(piece.astype(BF16), head_major(rows // heads, heads, 2))
    low = iota((cols // 2, 2 * rows), 1) < rows
    folded = jnp.where(low, moved[: cols // 2], moved[cols // 2 :]).astype(BF16)
    out_ref[...] = jnp.broadcast_to(folded[None], out_ref.shape)


def value_kernel(place_ref, scale_ref, quant_ref, out_ref):
    block, run = place_ref[0], place_ref[1]
    for h in range(quant_ref.shape[0]):
        out_ref[h ^ run] = (quant_ref[h].astype(F32) * scale_ref[block, h]).astype(BF16)


def ready_kernel(query_ref, key_ref, cache_ref, rope_ref, moved_ref):
    rows = query_ref.shape[0]
    latent = cache_ref.shape[1]
    drafts = rows // RUN
    query = dot(head_major(drafts, RUN, 1), query_ref[...], ((0,), (0,))).astype(BF16)
    rope_ref[...] = dot(query, key_ref[...])
    new = iota((latent, latent), 1)
    half, at = new // (latent // 2), new % (latent // 2)
    source = (at // 4) * 8 + half * 4 + at % 4
    order = (iota((latent, latent), 0) == source).astype(BF16)
    moved_ref[...] = dot(cache_ref[...], order).astype(BF16)


def split3(x):
    high = x.astype(BF16).astype(F32)
    middle = (x - high).astype(BF16).astype(F32)
    return high, middle, x - high - middle


def attend_kernel(factor, length_ref, start_ref, queries_ref, rope_ref, moved_ref, cache_ref, out_ref):
    rows, positions = rope_ref.shape
    senders, fold, _ = queries_ref.shape
    drafts = rows // RUN
    queries = queries_ref[...].reshape(senders * fold, 2 * rows)
    queries = jnp.concatenate([queries[:, :rows], queries[:, rows:]], axis=0)
    scores = (dot(queries, moved_ref[...], ((0,), (1,))) + rope_ref[...]) * factor
    position = start_ref[0] + iota(scores.shape, 1)
    visible = position < length_ref[0] + iota(scores.shape, 0) % drafts
    top = jnp.max(jnp.where(visible, scores, NEG), axis=1, keepdims=True)
    probs = jnp.where(visible, jnp.exp(scores - top), 0.0)
    total = jnp.sum(probs, axis=1, keepdims=True)
    out = dot(probs.astype(BF16), cache_ref[...])
    lane = iota((rows, LANES), 1)
    stats = jnp.zeros(lane.shape, F32)
    for k, part in enumerate((*split3(top), *split3(total))):
        stats = jnp.where(lane % 8 == k, part, stats)
    low = iota((2, LANES), 1) < 8
    for h in range(RUN):
        at = h * drafts
        both = jnp.where(low, stats[at : at + 2], stats[at + 2 : at + 4]).astype(BF16)
        for q in range(out_ref.shape[0] // RUN):
            columns = slice(q * LANES, (q + 1) * LANES)
            for k in range(drafts // 2):
                out_ref[q * RUN + h, k] = out[at + 2 * k : at + 2 * k + 2, columns].astype(BF16)
            out_ref[q * RUN + h, drafts // 2] = both


def head_kernel(run_ref, parts_ref, value_ref, out_ref):
    run = run_ref[0]
    pairs = parts_ref.shape[1] - 1
    stats = parts_ref[:, pairs].astype(F32)
    latents = []
    for k in range(pairs):
        tops, sums = (
            sum(stats[:, :, 8 * k + at + i : 8 * k + at + i + 1] for i in range(3)) for at in (0, 3)
        )
        shrink = jnp.exp(tops - jnp.max(tops, axis=0, keepdims=True))
        total = jnp.sum(sums * shrink, axis=0)
        merged = jnp.sum(parts_ref[:, k].astype(F32) * shrink, axis=0)
        latents.append(merged / total)
    latent = jnp.concatenate(latents, axis=0).astype(BF16)
    weight = jnp.concatenate([value_ref[j ^ run] for j in range(RUN)], axis=0)
    out_ref[...] = jnp.broadcast_to(dot(latent, weight).astype(BF16)[None], out_ref.shape)


def project_kernel(parts_ref, weight_ref, out_ref):
    devices = parts_ref.shape[0]
    heads = sum(parts_ref[q * RUN : (q + 1) * RUN].astype(F32) for q in range(devices // RUN)).astype(BF16)
    flat = jnp.concatenate([heads[h] for h in range(RUN)], axis=1)
    term = dot(flat, weight_ref[...], ((1,), (1,)))
    out_ref[...] = jnp.broadcast_to(term[None], out_ref.shape)


def call(kernel, shapes, specs, dtypes=BF16, scratch=()):
    if isinstance(dtypes, tuple):
        out_shape = [jax.ShapeDtypeStruct(s, d) for s, d in zip(shapes, dtypes)]
        out_specs = [VMEM] * len(shapes)
    else:
        out_shape, out_specs = jax.ShapeDtypeStruct(shapes, dtypes), VMEM
    return pl.pallas_call(
        kernel,
        out_shape=out_shape,
        in_specs=specs,
        out_specs=out_specs,
        scratch_shapes=scratch,
        compiler_params=pltpu.CompilerParams(vmem_limit_bytes=32 * 1024 * 1024),
    )


def exchange(blocks):
    blocks = blocks[None]
    for step in (8, 4, 2, 1):
        kept, sent = blocks[:, :step], blocks[:, step:]
        came = lax.ppermute(sent, "run", [(i, i ^ step) for i in range(RUN)])
        blocks = jnp.stack([kept, came], axis=0 if step == 8 else 1).reshape(-1, step, *blocks.shape[2:])
    return blocks[:, 0]


def per_device(
    query_nope,
    query_rope,
    latent_cache,
    rope_keys,
    lengths,
    key_quant,
    key_scale,
    value_quant,
    value_scale,
    out_weight,
):
    seq = ("quarter", "run")
    groups, quarters = lax.axis_size("heads"), lax.axis_size("quarter")
    devices = quarters * RUN
    _, drafts, heads, width = query_nope.shape
    rows = drafts * heads
    rope_width = query_rope.shape[3]
    _, positions, latent = latent_cache.shape
    cols = key_quant.shape[1]
    mine = out_weight.shape[1]
    run = lax.axis_index("run").astype(jnp.int32)
    place = lax.axis_index("quarter").astype(jnp.int32) * RUN + run
    block = (place * cols) >> 7
    start = place * positions
    factor = (width + rope_width) ** (-0.5)

    pieces = call(
        query_kernel,
        (devices, cols // 2, 2 * rows),
        [SMEM, HBM, HBM, HBM],
        scratch=(
            pltpu.SMEM(key_scale.T.shape, F32),
            pltpu.VMEM((rows, width), BF16),
            pltpu.VMEM(key_quant.shape, BF16),
            pltpu.SemaphoreType.DMA((3,)),
        ),
    )(block[None], key_scale.T, query_nope.reshape(rows, width), key_quant)
    queries = lax.all_to_all(pieces, seq, 0, 0, tiled=True)

    values = exchange(
        call(value_kernel, value_quant.shape, [SMEM, SMEM, VMEM])(
            jnp.stack([block, run]), value_scale.T, value_quant
        )
    )

    rope, moved = call(
        ready_kernel, ((rows, positions), (positions, latent)), [VMEM] * 3, (F32, BF16)
    )(query_rope.reshape(rows, rope_width), rope_keys[0], latent_cache[0])
    parts = call(
        lambda *refs: attend_kernel(factor, *refs),
        (devices, drafts // 2 + 1, 2, LANES),
        [SMEM, SMEM] + [VMEM] * 4,
    )(lengths, start[None], queries, rope, moved, latent_cache[0])
    parts = lax.all_to_all(parts, seq, 0, 0, tiled=True)

    terms = call(head_kernel, (devices, drafts, value_quant.shape[2]), [SMEM, VMEM, VMEM])(
        run[None], parts, values
    )
    terms = lax.all_to_all(terms, seq, 0, 0, tiled=True)
    sums = call(project_kernel, (groups, drafts, mine), [VMEM, VMEM], F32)(terms, out_weight.T)
    sums = lax.all_to_all(sums, "heads", 0, 0, tiled=True)
    return jnp.sum(sums, axis=0).astype(BF16)[None]


def solution(mesh):
    sizes = (mesh.shape["heads"], mesh.shape["seq"] // RUN, RUN)
    finer = Mesh(mesh.devices.reshape(sizes), ("heads", "quarter", "run"))
    seq = ("quarter", "run")
    in_specs = (
        P(None, None, "heads", None),
        P(None, None, "heads", None),
        P(None, seq, None),
        P(None, None, seq),
        P(),
        P("heads", seq, None),
        P("heads", None),
        P("heads", seq, None),
        P("heads", None),
        P("heads", seq),
    )
    out_specs = P(None, None, seq)
    return jax.shard_map(
        per_device, mesh=finer, in_specs=in_specs, out_specs=out_specs, check_vma=False
    )
```

```python
import jax
import jax.numpy as jnp
from jax import lax
from jax.experimental import pallas as pl
from jax.experimental.pallas import tpu as pltpu
from jax.sharding import PartitionSpec as P

QB = 128
HEADS = 16
FIRST = 34
LANES = 128
NEG = -1e30
F32 = jnp.float32
BF16 = jnp.bfloat16
SMEM = pl.BlockSpec(memory_space=pltpu.SMEM)
HBM = pl.BlockSpec(memory_space=pltpu.HBM)
VMEM = pl.BlockSpec(memory_space=pltpu.VMEM)


def iota(shape, dim):
    return lax.broadcasted_iota(jnp.int32, shape, dim)


def dot(a, b, dims=((1,), (0,))):
    return lax.dot_general(a, b, (dims, ((), ())), preferred_element_type=F32)


def head_major(drafts, heads, copies):
    rows = drafts * heads
    col = iota((rows, copies * rows), 1) % rows
    source = (col % drafts) * heads + col // drafts
    return (iota((rows, copies * rows), 0) == source).astype(BF16)


def message_kernel(block_ref, *refs):
    sources, out_ref, targets, sems = refs[:5], refs[5], refs[6:11], refs[11]
    copies = [pltpu.make_async_copy(*pair, sems.at[k]) for k, pair in enumerate(zip(sources, targets))]
    for copy in copies:
        copy.start()
    for copy in copies:
        copy.wait()
    key_ref, query_ref, value_ref, key_scale_ref, value_scale_ref = targets
    heads, cols, width = key_ref.shape
    rows = query_ref.shape[0]
    block = block_ref[0]
    weight = jnp.concatenate(
        [(key_ref[h].astype(F32) * key_scale_ref[block, h]).astype(BF16) for h in range(heads)], axis=0
    )
    both = dot(weight, query_ref[...], ((1,), (1,)))
    own = iota(both.shape, 0) // cols == iota(both.shape, 1) % heads
    piece = jnp.sum(jnp.where(own, both, 0.0).reshape(heads, cols, rows), axis=0)
    moved = dot(piece.astype(BF16), head_major(rows // heads, heads, cols // 2))
    kept = jnp.where(iota(moved.shape, 0) // 2 == iota(moved.shape, 1) // rows, moved, 0.0)
    folded = sum(kept[i : i + 2] for i in range(0, cols, 2)).astype(BF16)
    for k in range(2):
        tile = folded[:, k * LANES : (k + 1) * LANES]
        out_ref[:, k] = jnp.broadcast_to(tile[None], (out_ref.shape[0], 2, LANES))
    for h in range(heads):
        weight = value_ref[h].astype(F32) * value_scale_ref[block, h]
        for q in range(cols // 2):
            out_ref[q * heads + h, 2] = weight[2 * q : 2 * q + 2].astype(BF16)


def ready_kernel(query_ref, key_ref, cache_ref, rope_ref, moved_ref):
    rows = query_ref.shape[0]
    latent = cache_ref.shape[1]
    query = dot(head_major(rows // HEADS, HEADS, 1), query_ref[...], ((0,), (0,))).astype(BF16)
    rope_ref[...] = dot(query, key_ref[...])
    new = iota((latent, latent), 1)
    quarter, sender, j = new // LANES, new % LANES // 2, new % 2
    source = (sender + FIRST) % (LANES // 2) * 8 + quarter * 2 + j
    order = (iota((latent, latent), 0) == source).astype(BF16)
    moved_ref[...] = dot(cache_ref[...], order).astype(BF16)


def split3(x):
    high = x.astype(BF16).astype(F32)
    middle = (x - high).astype(BF16).astype(F32)
    return high, middle, x - high - middle


def tile_of(ref, k):
    return ref[:, k].reshape(2 * ref.shape[0], LANES)


def attend_kernel(factor, length_ref, start_ref, queries_ref, rope_ref, cache_ref, out_ref):
    rows, positions = rope_ref.shape
    drafts = rows // HEADS
    tiles = [tile_of(queries_ref, k) for k in range(2)]
    queries = jnp.concatenate([tile[:, at : at + rows] for tile in tiles for at in (0, rows)], axis=0)
    scores = (dot(queries, cache_ref[...], ((0,), (1,))) + rope_ref[...]) * factor
    position = start_ref[0] + iota(scores.shape, 1)
    visible = position < length_ref[0] + iota(scores.shape, 0) % drafts
    top = jnp.max(jnp.where(visible, scores, NEG), axis=1, keepdims=True)
    probs = jnp.where(visible, jnp.exp(scores - top), 0.0)
    total = jnp.sum(probs, axis=1, keepdims=True)
    out = dot(probs.astype(BF16), cache_ref[...])
    lane = iota((rows, LANES), 1)
    stats = jnp.zeros(lane.shape, F32)
    for k, part in enumerate((*split3(top), *split3(total))):
        stats = jnp.where(lane % 8 == k, part, stats)
    low = iota((2, LANES), 1) < 8
    for h in range(HEADS):
        at = h * drafts
        both = jnp.where(low, stats[at : at + 2], stats[at + 2 : at + 4]).astype(BF16)
        for q in range(out_ref.shape[0] // HEADS):
            columns = slice(q * LANES, (q + 1) * LANES)
            for k in range(drafts // 2):
                out_ref[q * HEADS + h, k] = out[at + 2 * k : at + 2 * k + 2, columns].astype(BF16)
            out_ref[q * HEADS + h, drafts // 2] = both


def head_kernel(parts_ref, queries_ref, out_ref):
    pairs = parts_ref.shape[1] - 1
    stats = parts_ref[:, pairs].astype(F32)
    latents = []
    for k in range(pairs):
        tops, sums = (
            sum(stats[:, :, 8 * k + at + i : 8 * k + at + i + 1] for i in range(3)) for at in (0, 3)
        )
        shrink = jnp.exp(tops - jnp.max(tops, axis=0, keepdims=True))
        total = jnp.sum(sums * shrink, axis=0)
        merged = jnp.sum(parts_ref[:, k].astype(F32) * shrink, axis=0)
        latents.append(merged / total)
    latent = jnp.concatenate(latents, axis=0).astype(BF16)
    out_ref[...] = jnp.broadcast_to(dot(latent, tile_of(queries_ref, 2)).astype(BF16)[None], out_ref.shape)


def project_kernel(parts_ref, weight_ref, out_ref):
    devices = parts_ref.shape[0]
    heads = sum(parts_ref[at : at + HEADS].astype(F32) for at in range(0, devices, HEADS)).astype(BF16)
    flat = jnp.concatenate([heads[h] for h in range(HEADS)], axis=1)
    term = dot(flat, weight_ref[...], ((1,), (1,)))
    out_ref[...] = jnp.broadcast_to(term[None], out_ref.shape)


def call(kernel, shapes, specs, dtypes=BF16, scratch=(), limit=32 * 1024 * 1024):
    if isinstance(dtypes, tuple):
        out_shape = [jax.ShapeDtypeStruct(s, d) for s, d in zip(shapes, dtypes)]
        out_specs = [VMEM] * len(shapes)
    else:
        out_shape, out_specs = jax.ShapeDtypeStruct(shapes, dtypes), VMEM
    return pl.pallas_call(
        kernel,
        out_shape=out_shape,
        in_specs=specs,
        out_specs=out_specs,
        scratch_shapes=scratch,
        compiler_params=pltpu.CompilerParams(vmem_limit_bytes=limit),
    )


def to_everyone(x, axis, first):
    size = lax.axis_size(axis)
    order = [(first + k) % size for k in range(size)]
    return lax.all_to_all(x, axis, 0, 0, tiled=True, axis_index_groups=[order])


def per_device(
    query_nope,
    query_rope,
    latent_cache,
    rope_keys,
    lengths,
    key_quant,
    key_scale,
    value_quant,
    value_scale,
    out_weight,
):
    groups, devices = lax.axis_size("heads"), lax.axis_size("seq")
    _, drafts, heads, width = query_nope.shape
    rows = drafts * heads
    rope_width = query_rope.shape[3]
    _, positions, latent = latent_cache.shape
    cols = key_quant.shape[1]
    place = lax.axis_index("seq").astype(jnp.int32)
    block = (place * cols) >> 7
    start = place * positions
    factor = (width + rope_width) ** (-0.5)
    tiles = (devices, 3, 2, LANES)

    messages = call(
        message_kernel,
        tiles,
        [SMEM] + [HBM] * 5,
        scratch=(
            pltpu.VMEM(key_quant.shape, BF16),
            pltpu.VMEM((rows, width), BF16),
            pltpu.VMEM(value_quant.shape, BF16),
            pltpu.SMEM(key_scale.T.shape, F32),
            pltpu.SMEM(value_scale.T.shape, F32),
            pltpu.SemaphoreType.DMA((5,)),
        ),
        limit=None,
    )(block[None], key_quant, query_nope.reshape(rows, width), value_quant, key_scale.T, value_scale.T)
    queries = to_everyone(messages, "seq", FIRST)

    rope, moved = call(
        ready_kernel, ((rows, positions), (positions, latent)), [VMEM] * 3, (F32, BF16)
    )(query_rope.reshape(rows, rope_width), rope_keys[0], latent_cache[0])
    parts = call(lambda *refs: attend_kernel(factor, *refs), tiles, [SMEM, SMEM] + [VMEM] * 3)(
        lengths, start[None], queries, rope, moved
    )
    parts = to_everyone(parts, "seq", FIRST)

    terms = call(head_kernel, (devices, drafts, value_quant.shape[2]), [VMEM, VMEM])(parts, queries)
    terms = to_everyone(terms, "seq", FIRST)
    sums = call(project_kernel, (groups, drafts, out_weight.shape[1]), [VMEM, VMEM], F32)(
        terms, out_weight.T
    )
    sums = to_everyone(sums, "heads", 0)
    return jnp.sum(sums, axis=0).astype(BF16)[None]


def solution(mesh):
    in_specs = (
        P(None, None, "heads", None),
        P(None, None, "heads", None),
        P(None, "seq", None),
        P(None, None, "seq"),
        P(),
        P("heads", "seq", None),
        P("heads", None),
        P("heads", "seq", None),
        P("heads", None),
        P("heads", "seq"),
    )
    out_specs = P(None, None, "seq")
    return jax.shard_map(
        per_device, mesh=mesh, in_specs=in_specs, out_specs=out_specs, check_vma=False
    )
```

```python
import jax
import jax.numpy as jnp
from jax import lax
from jax.experimental import pallas as pl
from jax.experimental.pallas import tpu as pltpu
from jax.sharding import PartitionSpec as P

QB = 128
HEADS = 16
FIRST = 35
LEADER = 5
LANES = 128
NEG = -1e30
F32 = jnp.float32
BF16 = jnp.bfloat16
SMEM = pl.BlockSpec(memory_space=pltpu.SMEM)
HBM = pl.BlockSpec(memory_space=pltpu.HBM)
VMEM = pl.BlockSpec(memory_space=pltpu.VMEM)


def iota(shape, dim):
    return lax.broadcasted_iota(jnp.int32, shape, dim)


def dot(a, b, dims=((1,), (0,))):
    return lax.dot_general(a, b, (dims, ((), ())), preferred_element_type=F32)


def head_major(drafts, heads, copies):
    rows = drafts * heads
    col = iota((rows, copies * rows), 1) % rows
    source = (col % drafts) * heads + col // drafts
    return (iota((rows, copies * rows), 0) == source).astype(BF16)


def message_kernel(*refs):
    sources, out_ref, targets, sems = refs[:5], refs[5], refs[6:11], refs[11]
    copies = [pltpu.make_async_copy(*pair, sems.at[k]) for k, pair in enumerate(zip(sources, targets))]
    for copy in copies:
        copy.start()
    for copy in copies:
        copy.wait()
    key_ref, query_ref, value_ref, key_scale_ref, value_scale_ref = targets
    heads, cols, width = key_ref.shape
    rows = query_ref.shape[0]
    block = lax.axis_index("seq") * cols // QB
    weight = jnp.concatenate(
        [(key_ref[h].astype(F32) * key_scale_ref[block, h]).astype(BF16) for h in range(heads)], axis=0
    )
    both = dot(weight, query_ref[...], ((1,), (1,)))
    own = iota(both.shape, 0) // cols == iota(both.shape, 1) % heads
    piece = jnp.sum(jnp.where(own, both, 0.0).reshape(heads, cols, rows), axis=0)
    moved = dot(piece.astype(BF16), head_major(rows // heads, heads, cols // 2))
    kept = jnp.where(iota(moved.shape, 0) // 2 == iota(moved.shape, 1) // rows, moved, 0.0)
    folded = sum(kept[i : i + 2] for i in range(0, cols, 2)).astype(BF16)
    for k in range(2):
        tile = folded[:, k * LANES : (k + 1) * LANES]
        out_ref[:, k] = jnp.broadcast_to(tile[None], (out_ref.shape[0], 2, LANES))
    for h in range(heads):
        weight = value_ref[h].astype(F32) * value_scale_ref[block, h]
        for q in range(cols // 2):
            out_ref[q * heads + h, 2] = weight[2 * q : 2 * q + 2].astype(BF16)


def ready_kernel(query_ref, key_ref, cache_ref, rope_ref, moved_ref):
    rows = query_ref.shape[0]
    latent = cache_ref.shape[1]
    query = dot(head_major(rows // HEADS, HEADS, 1), query_ref[...], ((0,), (0,))).astype(BF16)
    rope_ref[...] = dot(query, key_ref[...])
    new = iota((latent, latent), 1)
    quarter, sender, j = new // LANES, new % LANES // 2, new % 2
    source = (sender + FIRST) % (LANES // 2) * 8 + quarter * 2 + j
    order = (iota((latent, latent), 0) == source).astype(BF16)
    moved_ref[...] = dot(cache_ref[...], order).astype(BF16)


def split3(x):
    high = x.astype(BF16).astype(F32)
    middle = (x - high).astype(BF16).astype(F32)
    return high, middle, x - high - middle


def tile_of(ref, k):
    return ref[:, k].reshape(2 * ref.shape[0], LANES)


def attend_kernel(factor, length_ref, queries_ref, rope_ref, cache_ref, out_ref):
    rows, positions = rope_ref.shape
    drafts = rows // HEADS
    tiles = [tile_of(queries_ref, k) for k in range(2)]
    queries = jnp.concatenate([tile[:, at : at + rows] for tile in tiles for at in (0, rows)], axis=0)
    scores = (dot(queries, cache_ref[...], ((0,), (1,))) + rope_ref[...]) * factor
    position = lax.axis_index("seq") * positions + iota(scores.shape, 1)
    visible = position < length_ref[0] + iota(scores.shape, 0) % drafts
    top = jnp.max(jnp.where(visible, scores, NEG), axis=1, keepdims=True)
    probs = jnp.where(visible, jnp.exp(scores - top), 0.0)
    total = jnp.sum(probs, axis=1, keepdims=True)
    out = dot(probs.astype(BF16), cache_ref[...])
    lane = iota((rows, LANES), 1)
    stats = jnp.zeros(lane.shape, F32)
    for k, part in enumerate((*split3(top), *split3(total))):
        stats = jnp.where(lane % 8 == k, part, stats)
    low = iota((2, LANES), 1) < 8
    for h in range(HEADS):
        at = h * drafts
        both = jnp.where(low, stats[at : at + 2], stats[at + 2 : at + 4]).astype(BF16)
        for q in range(out_ref.shape[0] // HEADS):
            columns = slice(q * LANES, (q + 1) * LANES)
            for k in range(drafts // 2):
                out_ref[q * HEADS + h, k] = out[at + 2 * k : at + 2 * k + 2, columns].astype(BF16)
            out_ref[q * HEADS + h, drafts // 2] = both


def head_kernel(parts_ref, queries_ref, out_ref):
    pairs = parts_ref.shape[1] - 1
    stats = parts_ref[:, pairs].astype(F32)
    latents = []
    for k in range(pairs):
        tops, sums = (
            sum(stats[:, :, 8 * k + at + i : 8 * k + at + i + 1] for i in range(3)) for at in (0, 3)
        )
        shrink = jnp.exp(tops - jnp.max(tops, axis=0, keepdims=True))
        total = jnp.sum(sums * shrink, axis=0)
        merged = jnp.sum(parts_ref[:, k].astype(F32) * shrink, axis=0)
        latents.append(merged / total)
    latent = jnp.concatenate(latents, axis=0).astype(BF16)
    out_ref[...] = jnp.broadcast_to(dot(latent, tile_of(queries_ref, 2)).astype(BF16)[None], out_ref.shape)


def project_kernel(parts_ref, weight_ref, out_ref):
    devices = parts_ref.shape[0]
    heads = sum(parts_ref[at : at + HEADS].astype(F32) for at in range(0, devices, HEADS)).astype(BF16)
    flat = jnp.concatenate([heads[h] for h in range(HEADS)], axis=1)
    term = dot(flat, weight_ref[...], ((1,), (1,)))
    out_ref[...] = jnp.broadcast_to(term[None], out_ref.shape)


def call(kernel, shapes, specs, dtypes=BF16, scratch=(), limit=32 * 1024 * 1024):
    if isinstance(dtypes, tuple):
        out_shape = [jax.ShapeDtypeStruct(s, d) for s, d in zip(shapes, dtypes)]
        out_specs = [VMEM] * len(shapes)
    else:
        out_shape, out_specs = jax.ShapeDtypeStruct(shapes, dtypes), VMEM
    return pl.pallas_call(
        kernel,
        out_shape=out_shape,
        in_specs=specs,
        out_specs=out_specs,
        scratch_shapes=scratch,
        compiler_params=pltpu.CompilerParams(vmem_limit_bytes=limit),
    )


def to_everyone(x, axis, first):
    size = lax.axis_size(axis)
    order = [(first + k) % size for k in range(size)]
    return lax.all_to_all(x, axis, 0, 0, tiled=True, axis_index_groups=[order])


def per_device(
    query_nope,
    query_rope,
    latent_cache,
    rope_keys,
    lengths,
    key_quant,
    key_scale,
    value_quant,
    value_scale,
    out_weight,
):
    groups, devices = lax.axis_size("heads"), lax.axis_size("seq")
    _, drafts, heads, width = query_nope.shape
    rows = drafts * heads
    rope_width = query_rope.shape[3]
    _, positions, latent = latent_cache.shape
    factor = (width + rope_width) ** (-0.5)
    tiles = (devices, 3, 2, LANES)

    messages = call(
        message_kernel,
        tiles,
        [HBM] * 5,
        scratch=(
            pltpu.VMEM(key_quant.shape, BF16),
            pltpu.VMEM((rows, width), BF16),
            pltpu.VMEM(value_quant.shape, BF16),
            pltpu.SMEM(key_scale.T.shape, F32),
            pltpu.SMEM(value_scale.T.shape, F32),
            pltpu.SemaphoreType.DMA((5,)),
        ),
        limit=None,
    )(key_quant, query_nope.reshape(rows, width), value_quant, key_scale.T, value_scale.T)
    queries = to_everyone(messages, "seq", FIRST)

    rope, moved = call(
        ready_kernel, ((rows, positions), (positions, latent)), [VMEM] * 3, (F32, BF16)
    )(query_rope.reshape(rows, rope_width), rope_keys[0], latent_cache[0])
    parts = call(lambda *refs: attend_kernel(factor, *refs), tiles, [SMEM] + [VMEM] * 3)(
        lengths, queries, rope, moved
    )
    parts = to_everyone(parts, "seq", FIRST)

    terms = call(head_kernel, (devices, drafts, value_quant.shape[2]), [VMEM, VMEM])(parts, queries)
    terms = to_everyone(terms, "seq", FIRST)
    sums = call(project_kernel, (groups, drafts, out_weight.shape[1]), [VMEM, VMEM], F32)(
        terms, out_weight.T
    )
    sums = to_everyone(sums, "heads", LEADER)
    return jnp.sum(sums, axis=0).astype(BF16)[None]


def solution(mesh):
    in_specs = (
        P(None, None, "heads", None),
        P(None, None, "heads", None),
        P(None, "seq", None),
        P(None, None, "seq"),
        P(),
        P("heads", "seq", None),
        P("heads", None),
        P("heads", "seq", None),
        P("heads", None),
        P("heads", "seq"),
    )
    out_specs = P(None, None, "seq")
    return jax.shard_map(
        per_device, mesh=mesh, in_specs=in_specs, out_specs=out_specs, check_vma=False
    )
```

```python
import jax
import jax.numpy as jnp
from jax import lax
from jax.experimental import pallas as pl
from jax.experimental.pallas import tpu as pltpu
from jax.sharding import PartitionSpec as P

QB = 128
HEADS = 16
FIRST = 34
AHEAD = 1
LEADER = 5
LANES = 128
NEG = -1e30
F32 = jnp.float32
BF16 = jnp.bfloat16
SMEM = pl.BlockSpec(memory_space=pltpu.SMEM)
HBM = pl.BlockSpec(memory_space=pltpu.HBM)
VMEM = pl.BlockSpec(memory_space=pltpu.VMEM)


def iota(shape, dim):
    return lax.broadcasted_iota(jnp.int32, shape, dim)


def dot(a, b, dims=((1,), (0,))):
    return lax.dot_general(a, b, (dims, ((), ())), preferred_element_type=F32)


def place_of(quarter, head):
    return quarter * HEADS + head % (HEADS // 2) * 2 + head // (HEADS // 2)


def turn_of(quarter, head, devices):
    return (place_of(quarter, head) - AHEAD) % devices


def head_major(drafts, heads, copies):
    rows = drafts * heads
    col = iota((rows, copies * rows), 1) % rows
    source = (col % drafts) * heads + col // drafts
    return (iota((rows, copies * rows), 0) == source).astype(BF16)


def message_kernel(*refs):
    sources, out_ref, targets, sems = refs[:5], refs[5], refs[6:11], refs[11]
    copies = [pltpu.make_async_copy(*pair, sems.at[k]) for k, pair in enumerate(zip(sources, targets))]
    for copy in copies:
        copy.start()
    for copy in copies:
        copy.wait()
    key_ref, query_ref, value_ref, key_scale_ref, value_scale_ref = targets
    heads, cols, width = key_ref.shape
    rows = query_ref.shape[0]
    block = lax.axis_index("seq") * cols // QB
    weight = jnp.concatenate(
        [(key_ref[h].astype(F32) * key_scale_ref[block, h]).astype(BF16) for h in range(heads)], axis=0
    )
    both = dot(weight, query_ref[...], ((1,), (1,)))
    own = iota(both.shape, 0) // cols == iota(both.shape, 1) % heads
    piece = jnp.sum(jnp.where(own, both, 0.0).reshape(heads, cols, rows), axis=0)
    moved = dot(piece.astype(BF16), head_major(rows // heads, heads, cols // 2))
    kept = jnp.where(iota(moved.shape, 0) // 2 == iota(moved.shape, 1) // rows, moved, 0.0)
    folded = sum(kept[i : i + 2] for i in range(0, cols, 2)).astype(BF16)
    for k in range(2):
        tile = folded[:, k * LANES : (k + 1) * LANES]
        out_ref[:, k] = jnp.broadcast_to(tile[None], (out_ref.shape[0], 2, LANES))
    for h in range(heads):
        weight = value_ref[h].astype(F32) * value_scale_ref[block, h]
        for q in range(cols // 2):
            out_ref[turn_of(q, h, out_ref.shape[0]), 2] = weight[2 * q : 2 * q + 2].astype(BF16)


def ready_kernel(query_ref, key_ref, cache_ref, rope_ref, moved_ref):
    rows = query_ref.shape[0]
    latent = cache_ref.shape[1]
    query = dot(head_major(rows // HEADS, HEADS, 1), query_ref[...], ((0,), (0,))).astype(BF16)
    rope_ref[...] = dot(query, key_ref[...])
    new = iota((latent, latent), 1)
    quarter, sender, j = new // LANES, new % LANES // 2, new % 2
    source = (sender + FIRST + AHEAD) % (LANES // 2) * 8 + quarter * 2 + j
    order = (iota((latent, latent), 0) == source).astype(BF16)
    moved_ref[...] = dot(cache_ref[...], order).astype(BF16)


def split3(x):
    high = x.astype(BF16).astype(F32)
    middle = (x - high).astype(BF16).astype(F32)
    return high, middle, x - high - middle


def tile_of(ref, k):
    return ref[:, k].reshape(2 * ref.shape[0], LANES)


def attend_kernel(factor, length_ref, queries_ref, rope_ref, cache_ref, out_ref):
    rows, positions = rope_ref.shape
    drafts = rows // HEADS
    tiles = [tile_of(queries_ref, k) for k in range(2)]
    queries = jnp.concatenate([tile[:, at : at + rows] for tile in tiles for at in (0, rows)], axis=0)
    scores = (dot(queries, cache_ref[...], ((0,), (1,))) + rope_ref[...]) * factor
    position = lax.axis_index("seq") * positions + iota(scores.shape, 1)
    visible = position < length_ref[0] + iota(scores.shape, 0) % drafts
    top = jnp.max(jnp.where(visible, scores, NEG), axis=1, keepdims=True)
    probs = jnp.where(visible, jnp.exp(scores - top), 0.0)
    total = jnp.sum(probs, axis=1, keepdims=True)
    out = dot(probs.astype(BF16), cache_ref[...])
    lane = iota((rows, LANES), 1)
    stats = jnp.zeros(lane.shape, F32)
    for k, part in enumerate((*split3(top), *split3(total))):
        stats = jnp.where(lane % 8 == k, part, stats)
    low = iota((2, LANES), 1) < 8
    for h in range(HEADS):
        at = h * drafts
        both = jnp.where(low, stats[at : at + 2], stats[at + 2 : at + 4]).astype(BF16)
        for q in range(out_ref.shape[0] // HEADS):
            columns = slice(q * LANES, (q + 1) * LANES)
            turn = turn_of(q, h, out_ref.shape[0])
            for k in range(drafts // 2):
                out_ref[turn, k] = out[at + 2 * k : at + 2 * k + 2, columns].astype(BF16)
            out_ref[turn, drafts // 2] = both


def head_kernel(parts_ref, queries_ref, out_ref):
    pairs = parts_ref.shape[1] - 1
    stats = parts_ref[:, pairs].astype(F32)
    latents = []
    for k in range(pairs):
        tops, sums = (
            sum(stats[:, :, 8 * k + at + i : 8 * k + at + i + 1] for i in range(3)) for at in (0, 3)
        )
        shrink = jnp.exp(tops - jnp.max(tops, axis=0, keepdims=True))
        total = jnp.sum(sums * shrink, axis=0)
        merged = jnp.sum(parts_ref[:, k].astype(F32) * shrink, axis=0)
        latents.append(merged / total)
    latent = jnp.concatenate(latents, axis=0).astype(BF16)
    out_ref[...] = jnp.broadcast_to(dot(latent, tile_of(queries_ref, 2)).astype(BF16)[None], out_ref.shape)


def project_kernel(parts_ref, mine_ref, other_ref, out_ref):
    place = lax.axis_index("seq")
    half, core = (place + FIRST) % 2, place % 2
    count = HEADS // 2
    heads = sum(parts_ref[at : at + count].astype(F32) for at in range(0, parts_ref.shape[0], count)).astype(BF16)
    flat = jnp.concatenate([heads[h] for h in range(count)], axis=1)
    width = flat.shape[1]
    rows = pl.ds(pl.multiple_of(half * width, width), width)
    mine, other = (dot(flat, weight, ((1,), (1,))) for weight in (mine_ref[:, rows], other_ref[...]))
    for to in range(2):
        term = jnp.where(core == to, mine, other)
        for g in range(out_ref.shape[0] // 2):
            out_ref[2 * g + to] = term


def call(kernel, shapes, specs, dtypes=BF16, scratch=(), limit=32 * 1024 * 1024):
    if isinstance(dtypes, tuple):
        out_shape = [jax.ShapeDtypeStruct(s, d) for s, d in zip(shapes, dtypes)]
        out_specs = [VMEM] * len(shapes)
    else:
        out_shape, out_specs = jax.ShapeDtypeStruct(shapes, dtypes), VMEM
    return pl.pallas_call(
        kernel,
        out_shape=out_shape,
        in_specs=specs,
        out_specs=out_specs,
        scratch_shapes=scratch,
        compiler_params=pltpu.CompilerParams(vmem_limit_bytes=limit),
    )


def seq_order(devices, first, step=1):
    return [[(first + k) % devices for k in range(at, devices, step)] for at in range(step)]


def plane_order(groups, devices):
    return [
        [(LEADER + g) % groups * devices + at + core for g in range(groups) for core in range(2)]
        for at in range(0, devices, 2)
    ]


def to_everyone(x, axis, order):
    return lax.all_to_all(x, axis, 0, 0, tiled=True, axis_index_groups=order)


def per_device(
    query_nope,
    query_rope,
    latent_cache,
    rope_keys,
    lengths,
    key_quant,
    key_scale,
    value_quant,
    value_scale,
    out_weight,
):
    groups, devices = lax.axis_size("heads"), lax.axis_size("seq")
    _, drafts, heads, width = query_nope.shape
    rows = drafts * heads
    rope_width = query_rope.shape[3]
    _, positions, latent = latent_cache.shape
    factor = (width + rope_width) ** (-0.5)
    tiles = (devices, 3, 2, LANES)

    messages = call(
        message_kernel,
        tiles,
        [HBM] * 5,
        scratch=(
            pltpu.VMEM(key_quant.shape, BF16),
            pltpu.VMEM((rows, width), BF16),
            pltpu.VMEM(value_quant.shape, BF16),
            pltpu.SMEM(key_scale.T.shape, F32),
            pltpu.SMEM(value_scale.T.shape, F32),
            pltpu.SemaphoreType.DMA((5,)),
        ),
        limit=None,
    )(key_quant, query_nope.reshape(rows, width), value_quant, key_scale.T, value_scale.T)
    queries = to_everyone(messages, "seq", seq_order(devices, FIRST + AHEAD))

    rope, moved = call(
        ready_kernel, ((rows, positions), (positions, latent)), [VMEM] * 3, (F32, BF16)
    )(query_rope.reshape(rows, rope_width), rope_keys[0], latent_cache[0])
    mine, _ = lax.optimization_barrier((out_weight.T, rope))
    width = mine.shape[1] // 2
    mine = lax.dynamic_slice_in_dim(mine, (lax.axis_index("seq") + 1 + FIRST) % 2 * width, width, 1)
    other = lax.ppermute(mine, "seq", [(i, i ^ 1) for i in range(devices)])
    parts = call(lambda *refs: attend_kernel(factor, *refs), tiles, [SMEM] + [VMEM] * 3)(
        lengths, queries, rope, moved
    )
    parts, other = lax.optimization_barrier((parts, other))
    parts = to_everyone(parts, "seq", seq_order(devices, FIRST + AHEAD))

    terms = call(head_kernel, (devices // 2, drafts, value_quant.shape[2]), [VMEM, VMEM])(parts, queries)
    terms = to_everyone(terms, "seq", seq_order(devices, FIRST, 2))
    sums = call(project_kernel, (2 * groups, drafts, out_weight.shape[1]), [VMEM] * 3, F32)(
        terms, out_weight.T, other
    )
    sums = to_everyone(sums, ("heads", "seq"), plane_order(groups, devices))
    return jnp.sum(sums, axis=0).astype(BF16)[None]


def solution(mesh):
    in_specs = (
        P(None, None, "heads", None),
        P(None, None, "heads", None),
        P(None, "seq", None),
        P(None, None, "seq"),
        P(),
        P("heads", "seq", None),
        P("heads", None),
        P("heads", "seq", None),
        P("heads", None),
        P("heads", "seq"),
    )
    out_specs = P(None, None, "seq")
    return jax.shard_map(
        per_device, mesh=mesh, in_specs=in_specs, out_specs=out_specs, check_vma=False
    )
```

```python
import jax
import jax.numpy as jnp
from jax import lax
from jax.experimental import pallas as pl
from jax.experimental.pallas import tpu as pltpu
from jax.sharding import PartitionSpec as P

QB = 128
HEADS = 16
FIRST = 34
AHEAD = 1
LEADER = 5
LANES = 128
NEG = -1e30
F32 = jnp.float32
BF16 = jnp.bfloat16
SMEM = pl.BlockSpec(memory_space=pltpu.SMEM)
HBM = pl.BlockSpec(memory_space=pltpu.HBM)
VMEM = pl.BlockSpec(memory_space=pltpu.VMEM)


def iota(shape, dim):
    return lax.broadcasted_iota(jnp.int32, shape, dim)


def dot(a, b, dims=((1,), (0,))):
    return lax.dot_general(a, b, (dims, ((), ())), preferred_element_type=F32)


def place_of(quarter, head):
    return quarter * HEADS + head % (HEADS // 2) * 2 + head // (HEADS // 2)


def turn_of(quarter, head, devices):
    return (place_of(quarter, head) - AHEAD) % devices


def head_major(drafts, heads, copies):
    rows = drafts * heads
    col = iota((rows, copies * rows), 1) % rows
    source = (col % drafts) * heads + col // drafts
    return (iota((rows, copies * rows), 0) == source).astype(BF16)


def message_kernel(*refs):
    sources, out_ref, targets, sems = refs[:5], refs[5], refs[6:11], refs[11]
    copies = [pltpu.make_async_copy(*pair, sems.at[k]) for k, pair in enumerate(zip(sources, targets))]
    for copy in copies:
        copy.start()
    for copy in copies:
        copy.wait()
    key_ref, query_ref, value_ref, key_scale_ref, value_scale_ref = targets
    heads, cols, width = key_ref.shape
    rows = query_ref.shape[0]
    block = lax.axis_index("seq") * cols // QB
    weight = jnp.concatenate(
        [(key_ref[h].astype(F32) * key_scale_ref[block, h]).astype(BF16) for h in range(heads)], axis=0
    )
    both = dot(weight, query_ref[...], ((1,), (1,)))
    own = iota(both.shape, 0) // cols == iota(both.shape, 1) % heads
    piece = jnp.sum(jnp.where(own, both, 0.0).reshape(heads, cols, rows), axis=0)
    moved = dot(piece.astype(BF16), head_major(rows // heads, heads, cols // 2))
    kept = jnp.where(iota(moved.shape, 0) // 2 == iota(moved.shape, 1) // rows, moved, 0.0)
    folded = sum(kept[i : i + 2] for i in range(0, cols, 2)).astype(BF16)
    for k in range(2):
        tile = folded[:, k * LANES : (k + 1) * LANES]
        out_ref[:, k] = jnp.broadcast_to(tile[None], (out_ref.shape[0], 2, LANES))
    for h in range(heads):
        weight = value_ref[h].astype(F32) * value_scale_ref[block, h]
        for q in range(cols // 2):
            out_ref[turn_of(q, h, out_ref.shape[0]), 2] = weight[2 * q : 2 * q + 2].astype(BF16)


def ready_kernel(query_ref, key_ref, cache_ref, rope_ref, moved_ref):
    rows = query_ref.shape[0]
    latent = cache_ref.shape[1]
    query = dot(head_major(rows // HEADS, HEADS, 1), query_ref[...], ((0,), (0,))).astype(BF16)
    rope_ref[...] = dot(query, key_ref[...])
    new = iota((latent, latent), 1)
    quarter, sender, j = new // LANES, new % LANES // 2, new % 2
    source = (sender + FIRST + AHEAD) % (LANES // 2) * 8 + quarter * 2 + j
    order = (iota((latent, latent), 0) == source).astype(BF16)
    moved_ref[...] = dot(cache_ref[...], order).astype(BF16)


def split3(x):
    high = x.astype(BF16).astype(F32)
    middle = (x - high).astype(BF16).astype(F32)
    return high, middle, x - high - middle


def tile_of(ref, k):
    return ref[:, k].reshape(2 * ref.shape[0], LANES)


def attend_kernel(factor, length_ref, queries_ref, rope_ref, cache_ref, out_ref):
    rows, positions = rope_ref.shape
    drafts = rows // HEADS
    tiles = [tile_of(queries_ref, k) for k in range(2)]
    queries = jnp.concatenate([tile[:, at : at + rows] for tile in tiles for at in (0, rows)], axis=0)
    scores = (dot(queries, cache_ref[...], ((0,), (1,))) + rope_ref[...]) * factor
    position = lax.axis_index("seq") * positions + iota(scores.shape, 1)
    visible = position < length_ref[0] + iota(scores.shape, 0) % drafts
    top = jnp.max(jnp.where(visible, scores, NEG), axis=1, keepdims=True)
    probs = jnp.where(visible, jnp.exp(scores - top), 0.0)
    total = jnp.sum(probs, axis=1, keepdims=True)
    out = dot(probs.astype(BF16), cache_ref[...])
    lane = iota((rows, LANES), 1)
    stats = jnp.zeros(lane.shape, F32)
    for k, part in enumerate((*split3(top), *split3(total))):
        stats = jnp.where(lane % 8 == k, part, stats)
    low = iota((2, LANES), 1) < 8
    for h in range(HEADS):
        at = h * drafts
        both = jnp.where(low, stats[at : at + 2], stats[at + 2 : at + 4]).astype(BF16)
        for q in range(out_ref.shape[0] // HEADS):
            columns = slice(q * LANES, (q + 1) * LANES)
            turn = turn_of(q, h, out_ref.shape[0])
            for k in range(drafts // 2):
                out_ref[turn, k] = out[at + 2 * k : at + 2 * k + 2, columns].astype(BF16)
            out_ref[turn, drafts // 2] = both


def head_kernel(parts_ref, queries_ref, out_ref):
    pairs = parts_ref.shape[1] - 1
    stats = parts_ref[:, pairs].astype(F32)
    latents = []
    for k in range(pairs):
        tops, sums = (
            sum(stats[:, :, 8 * k + at + i : 8 * k + at + i + 1] for i in range(3)) for at in (0, 3)
        )
        shrink = jnp.exp(tops - jnp.max(tops, axis=0, keepdims=True))
        total = jnp.sum(sums * shrink, axis=0)
        merged = jnp.sum(parts_ref[:, k].astype(F32) * shrink, axis=0)
        latents.append(merged / total)
    latent = jnp.concatenate(latents, axis=0).astype(BF16)
    out_ref[...] = jnp.broadcast_to(dot(latent, tile_of(queries_ref, 2)).astype(BF16)[None], out_ref.shape)


def project_kernel(parts_ref, mine_ref, other_ref, out_ref):
    place = lax.axis_index("seq")
    half, core = (place + FIRST) % 2, place % 2
    count = HEADS // 2
    heads = sum(parts_ref[at : at + count].astype(F32) for at in range(0, parts_ref.shape[0], count)).astype(BF16)
    flat = jnp.concatenate([heads[h] for h in range(count)], axis=1)
    width = flat.shape[1]
    rows = pl.ds(pl.multiple_of(half * width, width), width)
    mine, other = (dot(flat, weight, ((1,), (1,))) for weight in (mine_ref[:, rows], other_ref[...]))
    for to in range(2):
        term = jnp.where(core == to, mine, other)
        for g in range(out_ref.shape[0] // 2):
            out_ref[2 * g + 1 - to] = term


def call(kernel, shapes, specs, dtypes=BF16, scratch=(), limit=32 * 1024 * 1024):
    if isinstance(dtypes, tuple):
        out_shape = [jax.ShapeDtypeStruct(s, d) for s, d in zip(shapes, dtypes)]
        out_specs = [VMEM] * len(shapes)
    else:
        out_shape, out_specs = jax.ShapeDtypeStruct(shapes, dtypes), VMEM
    return pl.pallas_call(
        kernel,
        out_shape=out_shape,
        in_specs=specs,
        out_specs=out_specs,
        scratch_shapes=scratch,
        compiler_params=pltpu.CompilerParams(vmem_limit_bytes=limit),
    )


def seq_order(devices, first, step=1):
    return [[(first + k) % devices for k in range(at, devices, step)] for at in range(step)]


def plane_order(groups, devices):
    return [
        [(LEADER + g) % groups * devices + at + core for g in range(groups) for core in (1, 0)]
        for at in range(0, devices, 2)
    ]


def to_everyone(x, axis, order):
    return lax.all_to_all(x, axis, 0, 0, tiled=True, axis_index_groups=order)


def per_device(
    query_nope,
    query_rope,
    latent_cache,
    rope_keys,
    lengths,
    key_quant,
    key_scale,
    value_quant,
    value_scale,
    out_weight,
):
    groups, devices = lax.axis_size("heads"), lax.axis_size("seq")
    _, drafts, heads, width = query_nope.shape
    rows = drafts * heads
    rope_width = query_rope.shape[3]
    _, positions, latent = latent_cache.shape
    factor = (width + rope_width) ** (-0.5)
    tiles = (devices, 3, 2, LANES)

    messages = call(
        message_kernel,
        tiles,
        [HBM] * 5,
        scratch=(
            pltpu.VMEM(key_quant.shape, BF16),
            pltpu.VMEM((rows, width), BF16),
            pltpu.VMEM(value_quant.shape, BF16),
            pltpu.SMEM(key_scale.T.shape, F32),
            pltpu.SMEM(value_scale.T.shape, F32),
            pltpu.SemaphoreType.DMA((5,)),
        ),
        limit=None,
    )(key_quant, query_nope.reshape(rows, width), value_quant, key_scale.T, value_scale.T)
    queries = to_everyone(messages, "seq", seq_order(devices, FIRST + AHEAD))

    rope, moved = call(
        ready_kernel, ((rows, positions), (positions, latent)), [VMEM] * 3, (F32, BF16)
    )(query_rope.reshape(rows, rope_width), rope_keys[0], latent_cache[0])
    mine, _ = lax.optimization_barrier((out_weight.T, rope))
    width = mine.shape[1] // 2
    mine = lax.dynamic_slice_in_dim(mine, (lax.axis_index("seq") + 1 + FIRST) % 2 * width, width, 1)
    other = lax.ppermute(mine, "seq", [(i, i ^ 1) for i in range(devices)])
    parts = call(lambda *refs: attend_kernel(factor, *refs), tiles, [SMEM] + [VMEM] * 3)(
        lengths, queries, rope, moved
    )
    parts, other = lax.optimization_barrier((parts, other))
    parts = to_everyone(parts, "seq", seq_order(devices, FIRST + AHEAD))

    terms = call(head_kernel, (devices // 2, drafts, value_quant.shape[2]), [VMEM, VMEM])(parts, queries)
    terms = to_everyone(terms, "seq", seq_order(devices, FIRST, 2))
    sums = call(project_kernel, (2 * groups, drafts, out_weight.shape[1]), [VMEM] * 3, F32)(
        terms, out_weight.T, other
    )
    sums = to_everyone(sums, ("heads", "seq"), plane_order(groups, devices))
    return jnp.sum(sums, axis=0).astype(BF16)[None]


def solution(mesh):
    in_specs = (
        P(None, None, "heads", None),
        P(None, None, "heads", None),
        P(None, "seq", None),
        P(None, None, "seq"),
        P(),
        P("heads", "seq", None),
        P("heads", None),
        P("heads", "seq", None),
        P("heads", None),
        P("heads", "seq"),
    )
    out_specs = P(None, None, "seq")
    return jax.shard_map(
        per_device, mesh=mesh, in_specs=in_specs, out_specs=out_specs, check_vma=False
    )
```
